256 devices in a mesh: wide: 32 (over z, y_lo, core), narrow: 8 (over y_hi, x).
Axes of the slice: x: 4, y: 4 (y_hi: 2, y_lo: 2; y = y_hi * 2 + y_lo), z: 8, core: 2. Of those that a mesh axis runs over, the one named last changes fastest.
Arguments:
- samples: bfloat16 [1536, 2048], P('wide', 'narrow'), may hold values from -6 to 6
- inverse_factors: bfloat16 [128, 2048, 2048], P('wide', 'narrow'), as said below
- offsets: float32 [128, 2048], P('wide', 'narrow'), may hold values from -1.2 to 1.2
- log_weights: float32 [128], P('wide'), may hold values from -3 to 3
Outputs:
- log_norm: float32 [1536], P('wide')
- means: float32 [128, 2048], P('wide', 'narrow')
- covariance: bfloat16 [128, 2048, 2048], P('wide', 'narrow')
The draws below stay inside these ranges and needn't reach their ends.
Inputs may be any that keep to these rules, and one draw needn't show every extreme that they name: `inverse_factors`: each component's factor is lower triangular, its diagonal entries from about 0.12 to 0.18.
All inputs are finite; a program needn't handle non-finite values.
Results may differ from the reference program's by a relative error of at most 0.0095.
Values may be sent and summed in bfloat16 or wider, within the bound.
No kernel may reach another device: no remote copies, remote signals or barrier semaphores. Data moves between devices by JAX's collectives and lax.ppermute only.
A program may use at most 128 MiB of HBM per device.

```python
import math
import jax
import jax.numpy as jnp
from jax import lax

F = 2048
K = 128
ROWS = 1536


def draw_inverse_factors(key, part):
    key = jax.random.fold_in(key, 7)
    key_off, key_diag = jax.random.split(key)
    row_ids = lax.broadcasted_iota(jnp.int32, (K, F, F), 1)
    col_ids = lax.broadcasted_iota(jnp.int32, (K, F, F), 2)
    lower = jax.random.truncated_normal(key_off, -4.0, 4.0, (K, F, F), jnp.float32)
    diagonal_vals = jax.random.uniform(key_diag, (K, F, F), jnp.float32, 0.125, 0.175)
    scale_off = 0.25 / math.sqrt(F)
    factor = jnp.where(col_ids < row_ids, lower * scale_off, jnp.where(col_ids == row_ids, diagonal_vals, 0.0))
    return factor.astype(jnp.bfloat16)


def levels(stream_key, extent, cuts, low, high):
    level = 1.0
    for axis_at, parts in cuts:
        draws = jax.random.uniform(jax.random.fold_in(jax.random.fold_in(stream_key, 6), axis_at), (parts,), jnp.float32, low / len(cuts), high / len(cuts))
        level = level * jnp.repeat(jnp.exp(draws), extent[axis_at] // parts).reshape((-1,) + (1,) * (len(extent) - 1 - axis_at))
    return level


def scatter_about(own_key, dims, deviation, most, cuts=(), dtype=jnp.bfloat16):
    result = deviation * jax.random.normal(own_key, dims, jnp.float32)
    if cuts:
        result = result * levels(own_key, dims, cuts, -0.22, 0.18)
    return jnp.clip(result, -most, most).astype(dtype)


def setup_inputs(seed: int = 0) -> dict:
    keys = jax.random.split(jax.random.key(seed), 5)
    return {
        "samples": scatter_about(keys[0], (ROWS, F), 1.0, 6.0, ((0, 32), (1, 8))),
        "inverse_factors": draw_inverse_factors(jax.random.fold_in(keys[4], 71), 0),
        "offsets": scatter_about(keys[2], (K, F), 0.2, 1.2, ((0, 32), (1, 8)), jnp.float32),
        "log_weights": scatter_about(keys[3], (K,), 1.0, 3.0, ((0, 32),), jnp.float32),
    }


def reference(samples, inverse_factors, offsets, log_weights):
    def component(pair):
        factor, offset = pair
        projected = jnp.dot(samples, factor.T, preferred_element_type=jnp.float32)
        centered = projected - offset[None, :]
        quadratic = jnp.sum(centered * centered, axis=1)
        log_det = jnp.sum(jnp.log(jnp.diagonal(factor).astype(jnp.float32)))
        return log_det - 0.5 * quadratic

    scores = lax.map(component, (inverse_factors, offsets))
    loglik = scores.T + log_weights[None, :]
    row_peak = jnp.max(loglik, axis=1)
    shifted = loglik - row_peak[:, None]
    log_norm = jnp.log(jnp.sum(jnp.exp(shifted), axis=1))
    responsibility = jnp.exp(shifted - log_norm[:, None])
    counts = jnp.sum(responsibility, axis=0)
    sums = jnp.dot(responsibility.T, samples.astype(jnp.float32), precision=lax.Precision.HIGHEST)
    inverse_count = 1.0 / (counts + 1.0)
    means = sums * inverse_count[:, None]

    def second_moment(triple):
        weight_col, mean_row, inverse_one = triple
        weighted = (weight_col[:, None] * samples.astype(jnp.float32)).astype(jnp.bfloat16)
        gram = jnp.dot(weighted.T, samples, preferred_element_type=jnp.float32)
        return (gram * inverse_one - mean_row[:, None] * mean_row[None, :]).astype(jnp.bfloat16)

    covariance = lax.map(second_moment, (responsibility.T, means, inverse_count))
    return log_norm, means, covariance
```

```python
import functools

import jax
import jax.numpy as jnp
from jax import lax
from jax.experimental import pallas as pl
from jax.experimental.pallas import tpu as pltpu
from jax.sharding import PartitionSpec as P

AXES = ("wide", "narrow")
NZ, NY, NX = 8, 4, 4


def linear(z, y, x, c):
    return ((z * 2 + y % 2) * 2 + c) * 8 + (y // 2) * 4 + x


def pairs(move):
    out = []
    for z in range(NZ):
        for y in range(NY):
            for x in range(NX):
                for c in range(2):
                    tz, ty, tx, tc = move(z, y, x, c)
                    out.append((linear(z, y, x, c), linear(tz % NZ, ty % NY, tx % NX, tc)))
    return out


def send(value, move):
    return lax.ppermute(value, AXES, pairs(move))


def z_step(d):
    return lambda z, y, x, c: (z + d, y, x, c)


def first_step(d):
    return lambda z, y, x, c: (z, y + d, x, c) if c == 0 else (z, y, x + d, c)


def second_step(d):
    return lambda z, y, x, c: (z, y, x + d, c) if c == 0 else (z, y + d, x, c)


def core_swap(z, y, x, c):
    return (z, y, x, 1 - c)


def place():
    w, n = lax.axis_index("wide"), lax.axis_index("narrow")
    return w // 4, (n // 4) * 2 + (w // 2) % 2, n % 4, w % 2


def gather(samples):
    z, y, x, c = place()
    up = [samples]
    down = [samples]
    for _ in range(3):
        up.append(send(up[-1], z_step(1)))
        down.append(send(down[-1], z_step(-1)))
    far = send(down[-1], z_step(-1))
    ring = jnp.stack([samples, down[1], down[2], down[3], far, up[3], up[2], up[1]])
    ring = jnp.concatenate([ring, ring], axis=0)
    column = lax.dynamic_slice_in_dim(ring, NZ - z, NZ, 0)
    before = send(column, first_step(1))
    after = send(column, first_step(-1))
    far_lo = send(before[: NZ // 2], first_step(1))
    far_hi = send(after[NZ // 2 :], first_step(-1))
    plane = jnp.stack([column, after, jnp.concatenate([far_lo, far_hi], axis=0), before])
    plane_before = send(plane, second_step(1))
    plane_after = send(plane, second_step(-1))
    plane_lo = send(plane_before[:2], second_step(1))
    plane_hi = send(plane_after[2:], second_step(-1))
    mine = [plane, plane_after, plane_lo, plane_hi, plane_before]
    return mine, [send(part, core_swap) for part in mine]


PARTS = ((0, 0, 4), (1, 0, 4), (2, 0, 2), (2, 2, 2), (3, 0, 4))


def score_kernel(spot, offsets_ref, factors_ref, *refs):
    parts, (partial_ref, rows_out, rows, sems, out_sem) = refs[:10], refs[10:]
    here_y, here_x, here_c, block = spot[0], spot[1], spot[2], spot[3]
    copies = []
    count = 0
    blocks = rows.reshape(NZ, 4, 48, rows.shape[1])
    for half in range(2):
        core = here_c if half == 0 else 1 - here_c
        for part, (second, first, many) in zip(parts[half * 5 : half * 5 + 5], PARTS, strict=True):
            for i in range(many):
                ay, ax = (here_y + first + i) % 4, (here_x + second) % 4
                by, bx = (here_y + second) % 4, (here_x + first + i) % 4
                at_y = jnp.where(core == 0, ay, by)
                at_x = jnp.where(core == 0, ax, bx)
                col = pl.multiple_of(((at_y // 2) * 4 + at_x) * 256, 256)
                slot = (at_y % 2) * 2 + core
                copy = pltpu.make_async_copy(
                    part.at[i], blocks.at[:, slot, :, pl.ds(col, 256)], sems.at[count]
                )
                copy.start()
                copies.append(copy)
                count += 1
    comps, span, feats = factors_ref.shape
    own = pl.multiple_of(block * span, span)
    eye = lax.broadcasted_iota(jnp.int32, (span, span), 0) == lax.broadcasted_iota(
        jnp.int32, (span, span), 1
    )
    log_dets = []
    for k in range(comps):
        square = factors_ref[k, :, pl.ds(own, span)].astype(jnp.float32)
        diag = jnp.sum(jnp.where(eye, square, 0.0), axis=1, keepdims=True)
        log_dets.append(jnp.sum(jnp.log(diag), axis=0, keepdims=True))
    for copy in copies:
        copy.wait()
    out_copy = pltpu.make_async_copy(rows, rows_out, out_sem)
    out_copy.start()
    tile = 256

    def score(t, carry):
        at = pl.multiple_of(t * tile, tile)
        chunk = rows[pl.ds(at, tile), :]
        projected = lax.dot_general(
            factors_ref[...].reshape(comps * span, feats),
            chunk,
            (((1,), (1,)), ((), ())),
            preferred_element_type=jnp.float32,
        )
        lines = []
        for k in range(comps):
            centered = projected[k * span : (k + 1) * span] - offsets_ref[k]
            quadratic = jnp.sum(centered * centered, axis=0, keepdims=True)
            lines.append(log_dets[k] - 0.5 * quadratic)
        partial_ref[:, pl.ds(at, tile)] = jnp.concatenate(lines, axis=0)
        return carry

    lax.fori_loop(0, rows.shape[0] // tile, score, 0)
    out_copy.wait()


def scores(spot, offsets, factors, parts):
    comps, span, feats = factors.shape
    total = 1536
    anywhere = pl.BlockSpec(memory_space=pl.ANY)
    whole = pl.BlockSpec(memory_space=pltpu.VMEM)
    return pl.pallas_call(
        score_kernel,
        out_shape=(
            jax.ShapeDtypeStruct((comps, total), jnp.float32),
            jax.ShapeDtypeStruct((total, feats), jnp.bfloat16),
        ),
        in_specs=[pl.BlockSpec(memory_space=pltpu.SMEM), whole, whole] + [anywhere] * 10,
        out_specs=(whole, anywhere),
        scratch_shapes=[
            pltpu.VMEM((total, feats), jnp.bfloat16),
            pltpu.SemaphoreType.DMA((32,)),
            pltpu.SemaphoreType.DMA,
        ],
        compiler_params=pltpu.CompilerParams(vmem_limit_bytes=40 * 2**20),
        name="scores",
    )(spot, offsets[:, :, None], factors, *parts)


def moment_kernel(spot, resp_ref, own_ref, rows_ref, means_ref, cov_ref, left, own_means, inverse):
    step = pl.program_id(0)
    comps, total = resp_ref.shape
    span = own_ref.shape[1]

    @pl.when(step == 0)
    def _():
        own_t = own_ref[...].T.astype(jnp.float32)
        resp = resp_ref[...]
        inv = 1.0 / (jnp.sum(resp, axis=1, keepdims=True) + 1.0)
        inverse[...] = jnp.broadcast_to(inv, inverse.shape)
        high = resp.astype(jnp.bfloat16)
        low = (resp - high.astype(jnp.float32)).astype(jnp.bfloat16)
        zero = jnp.zeros((8, total), jnp.bfloat16)
        left[pl.ds(comps * span, 16), :] = jnp.concatenate([high, low, zero], axis=0)
        for k in range(comps):
            weighted = own_t * resp[k : k + 1]
            left[pl.ds(k * span, span), :] = weighted.astype(jnp.bfloat16)
            own_means[k] = jnp.sum(weighted, axis=1, keepdims=True) * inv[k : k + 1]

    gram = jnp.dot(left[...], rows_ref[...], preferred_element_type=jnp.float32)
    sums = gram[comps * span : comps * span + comps] + gram[comps * span + comps : comps * span + 2 * comps]
    means = sums * inverse[:, 0:1]

    @pl.when(step == spot[3])
    def _():
        means_ref[...] = means

    for k in range(comps):
        cov_ref[k] = (
            gram[k * span : (k + 1) * span] * inverse[k : k + 1, 0:1] - own_means[k] * means[k : k + 1]
        ).astype(jnp.bfloat16)


def moments(spot, resp, rows, span):
    comps, total = resp.shape
    feats = rows.shape[1]
    tile = 256
    grid_spec = pltpu.PrefetchScalarGridSpec(
        num_scalar_prefetch=1,
        grid=(feats // tile,),
        in_specs=[
            pl.BlockSpec((comps, total), lambda t, spot: (0, 0)),
            pl.BlockSpec((total, span), lambda t, spot: (0, spot[3])),
            pl.BlockSpec((total, tile), lambda t, spot: (0, t)),
        ],
        out_specs=(
            pl.BlockSpec((comps, tile), lambda t, spot: (0, 0)),
            pl.BlockSpec((comps, span, tile), lambda t, spot: (0, 0, t)),
        ),
        scratch_shapes=[
            pltpu.VMEM((comps * span + 16, total), jnp.bfloat16),
            pltpu.VMEM((comps, span, 1), jnp.float32),
            pltpu.VMEM((comps, 128), jnp.float32),
        ],
    )
    return pl.pallas_call(
        moment_kernel,
        grid_spec=grid_spec,
        out_shape=(
            jax.ShapeDtypeStruct((comps, span), jnp.float32),
            jax.ShapeDtypeStruct((comps, span, feats), jnp.bfloat16),
        ),
        compiler_params=pltpu.CompilerParams(vmem_limit_bytes=40 * 2**20),
        name="moments",
    )(spot, resp, rows, rows)


def mirror(x):
    return x ^ 1


def x_even(z, y, x, c):
    return (z, y, x ^ 1, c)


def x_odd(z, y, x, c):
    return (z, y, 3 - x, c)


def y_far(z, y, x, c):
    return (z, y + 2, x, c)


def y_near(z, y, x, c):
    return (z, y ^ 1, x, c)


def z_even(z, y, x, c):
    return (z ^ 1, y, x, c)


def z_odd(z, y, x, c):
    return (z + 1 if z % 2 else z - 1, y, x, c)


Z_LAST = {1: 6, 6: 1, 2: 5, 5: 2, 3: 0, 0: 3, 4: 7, 7: 4}


def z_far(z, y, x, c):
    return (Z_LAST[z], y, x, c)


def shards(samples, inverse_factors, offsets, log_weights):
    z, y, x, c = place()
    rows_here = samples.shape[0]
    spot = jnp.stack([y, x, c, lax.axis_index("narrow")]).astype(jnp.int32)
    mine, theirs = gather(samples)
    loglik, rows = scores(spot, offsets, inverse_factors, mine + theirs)
    for move in (x_even, x_odd, y_far):
        loglik = loglik + send(loglik, move)
    loglik = loglik + log_weights[:, None]
    peak = jnp.max(loglik, axis=0)
    total = jnp.sum(jnp.exp(loglik - peak[None, :]), axis=0)
    pair = jnp.stack([peak, total])
    for move in (core_swap, y_near, z_even, z_odd, z_far):
        other = send(pair, move)
        peak = jnp.maximum(pair[0], other[0])
        total = pair[1] * jnp.exp(pair[0] - peak) + other[1] * jnp.exp(other[0] - peak)
        pair = jnp.stack([peak, total])
    log_norm = jnp.log(pair[1])
    responsibility = jnp.exp((loglik - pair[0][None, :]) - log_norm[None, :])
    means, covariance = moments(spot, responsibility, rows, inverse_factors.shape[1])
    own_norm = lax.dynamic_slice_in_dim(log_norm, lax.axis_index("wide") * rows_here, rows_here, 0)
    return (own_norm, means, covariance)


def solution(mesh):
    return jax.shard_map(
        shards,
        mesh=mesh,
        in_specs=(P("wide", "narrow"), P("wide", "narrow", None), P("wide", "narrow"), P("wide")),
        out_specs=(P("wide"), P("wide", "narrow"), P("wide", "narrow", None)),
        check_vma=False,
    )
```

```python
import functools

import jax
import jax.numpy as jnp
from jax import lax
from jax.experimental import pallas as pl
from jax.experimental.pallas import tpu as pltpu
from jax.sharding import PartitionSpec as P

AXES = ("wide", "narrow")
NZ, NY, NX = 8, 4, 4


def linear(z, y, x, c):
    return ((z * 2 + y % 2) * 2 + c) * 8 + (y // 2) * 4 + x


def pairs(move):
    out = []
    for z in range(NZ):
        for y in range(NY):
            for x in range(NX):
                for c in range(2):
                    tz, ty, tx, tc = move(z, y, x, c)
                    out.append((linear(z, y, x, c), linear(tz % NZ, ty % NY, tx % NX, tc)))
    return out


def send(value, move):
    return lax.ppermute(value, AXES, pairs(move))


def z_step(d):
    return lambda z, y, x, c: (z + d, y, x, c)


def first_step(d):
    return lambda z, y, x, c: (z, y + d, x, c) if c == 0 else (z, y, x + d, c)


def second_step(d):
    return lambda z, y, x, c: (z, y, x + d, c) if c == 0 else (z, y + d, x, c)


def core_swap(z, y, x, c):
    return (z, y, x, 1 - c)


def place():
    w, n = lax.axis_index("wide"), lax.axis_index("narrow")
    return w // 4, (n // 4) * 2 + (w // 2) % 2, n % 4, w % 2


def column_kernel(spot, *refs):
    out_ref = refs[-1]
    for i, ref in enumerate(refs[:-1]):
        out_ref[(spot[4] + i) % NZ] = ref[...]


def make_column(spot, ring):
    return pl.pallas_call(
        column_kernel,
        out_shape=pltpu.VMEM((NZ,) + ring[0].shape, ring[0].dtype),
        in_specs=[SMEM] + [VMEM] * NZ,
        out_specs=VMEM,
        compiler_params=pltpu.CompilerParams(vmem_limit_bytes=2 * 2**20),
        name="column",
    )(spot, *ring)


def gather(spot, samples, log_det):
    back, ahead, back2, ahead2 = (send(samples, z_step(d)) for d in (1, -1, 2, -2))
    ahead3, back3, far = send(ahead2, z_step(-1)), send(back2, z_step(1)), send(ahead2, z_step(-2))
    column = make_column(spot, [samples, ahead, ahead2, ahead3, far, back3, back2, back])
    before, after, across = (send(column, first_step(d)) for d in (1, -1, 2))
    plane = jnp.stack([column, after, across, before])
    low, high = plane[:2], plane[2:]
    before_low = send(low, second_step(1))
    after_high = send(high, second_step(-1))
    before_high = send(high, second_step(1))
    after_low = send(low, second_step(-1))
    far_low = send(before_low, second_step(1))
    far_high = send(after_high, second_step(-1))
    plane, log_det = lax.optimization_barrier((plane, log_det))
    near = [plane, before_low, after_high, before_high, after_low]
    return lay(spot, FAR, lay(spot, NEAR, None, near), [far_low, far_high]), log_det


NEAR = ((0, 0, 4), (3, 0, 2), (1, 2, 2), (3, 2, 2), (1, 0, 2))
FAR = ((2, 0, 2), (2, 2, 2))
VMEM = pl.BlockSpec(memory_space=pltpu.VMEM)
ANY = pl.BlockSpec(memory_space=pl.ANY)
SMEM = pl.BlockSpec(memory_space=pltpu.SMEM)


def lay_kernel(places, has_rows, spot, *refs):
    parts = refs[has_rows : has_rows + len(places)]
    rows, sems = refs[-2:]
    here_y, here_x = spot[0], spot[1]
    core = spot[2]
    blocks = rows.reshape(NZ, 2, 48, rows.shape[1])
    copies = []
    for part, (second, first, many) in zip(parts, places, strict=True):
        for i in range(many):
            ay, ax = (here_y + first + i) % 4, (here_x + second) % 4
            by, bx = (here_y + second) % 4, (here_x + first + i) % 4
            at_y = jnp.where(core == 0, ay, by)
            at_x = jnp.where(core == 0, ax, bx)
            col = pl.multiple_of(((at_y // 2) * 4 + at_x) * 256, 256)
            copy = pltpu.make_async_copy(
                part.at[i], blocks.at[:, at_y % 2, :, pl.ds(col, 256)], sems.at[len(copies)]
            )
            copy.start()
            copies.append(copy)
    for copy in copies:
        copy.wait()


def lay(spot, places, rows, parts):
    has_rows = 0 if rows is None else 1
    return pl.pallas_call(
        functools.partial(lay_kernel, places, has_rows),
        out_shape=pltpu.VMEM((768, 2048), jnp.bfloat16),
        in_specs=[SMEM] + [VMEM] * has_rows + [ANY] * len(parts),
        out_specs=VMEM,
        scratch_shapes=[pltpu.SemaphoreType.DMA((12,))],
        input_output_aliases={1: 0} if has_rows else {},
        compiler_params=pltpu.CompilerParams(vmem_limit_bytes=2 * 2**20),
        name="lay",
    )(spot, *([rows] if has_rows else []), *parts)


def log_det_kernel(spot, factors_ref, log_det_ref, square, sem):
    comps, span, _ = factors_ref.shape
    own = pl.multiple_of(spot[3] * span, span)
    copy = pltpu.make_async_copy(factors_ref.at[:, :, pl.ds(own, span)], square, sem)
    copy.start()
    eye = lax.broadcasted_iota(jnp.int32, (span, span), 0) == lax.broadcasted_iota(
        jnp.int32, (span, span), 1
    )
    copy.wait()
    for k in range(comps):
        diag = jnp.sum(jnp.where(eye, square[k].astype(jnp.float32), 0.0), axis=1, keepdims=True)
        total = jnp.sum(jnp.log(diag), axis=0, keepdims=True)
        log_det_ref[k : k + 1, :] = jnp.broadcast_to(total, (1, log_det_ref.shape[1]))


def log_dets(spot, factors):
    comps, span, _ = factors.shape
    return pl.pallas_call(
        log_det_kernel,
        out_shape=jax.ShapeDtypeStruct((comps, 128), jnp.float32),
        in_specs=[SMEM, ANY],
        out_specs=VMEM,
        scratch_shapes=[pltpu.VMEM((comps, span, span), factors.dtype), pltpu.SemaphoreType.DMA],
        compiler_params=pltpu.CompilerParams(vmem_limit_bytes=4 * 2**20),
        name="log_dets",
    )(spot, factors)


def score_kernel(offsets_ref, log_det_ref, factors_ref, rows_ref, partial_ref):
    comps, span, feats = factors_ref.shape
    offsets = offsets_ref[...].T
    projected = lax.dot_general(
        factors_ref[...].reshape(comps * span, feats),
        rows_ref[...],
        (((1,), (1,)), ((), ())),
        preferred_element_type=jnp.float32,
    )
    for k in range(comps):
        centered = projected[k * span : (k + 1) * span] - offsets[:, k : k + 1]
        quadratic = jnp.sum(centered * centered, axis=0, keepdims=True)
        partial_ref[k : k + 1, :] = log_det_ref[k : k + 1, 0:1] - 0.5 * quadratic


def score(offsets, log_det, factors, rows):
    comps, span, feats = factors.shape
    total = rows.shape[0]
    return pl.pallas_call(
        score_kernel,
        out_shape=jax.ShapeDtypeStruct((comps, total), jnp.float32),
        in_specs=[VMEM, VMEM, VMEM, VMEM],
        out_specs=VMEM,
        compiler_params=pltpu.CompilerParams(vmem_limit_bytes=10 * 2**20),
        cost_estimate=pl.CostEstimate(
            flops=2 * total * comps * span * feats, bytes_accessed=8 * 2**20, transcendentals=0
        ),
        name="score",
    )(offsets, log_det, factors, rows)


def score_moved_kernel(offsets_ref, log_det_ref, factors_ref, rows_ref, partial_ref, held, sem):
    copy = pltpu.make_async_copy(rows_ref, held, sem)
    copy.start()
    copy.wait()
    score_kernel(offsets_ref, log_det_ref, factors_ref, held, partial_ref)


def score_moved(offsets, log_det, factors, rows):
    comps, span, feats = factors.shape
    total = rows.shape[0]
    return pl.pallas_call(
        score_moved_kernel,
        out_shape=(
            jax.ShapeDtypeStruct((comps, total), jnp.float32),
            pltpu.VMEM(rows.shape, rows.dtype),
        ),
        in_specs=[VMEM, VMEM, VMEM, ANY],
        out_specs=(VMEM, VMEM),
        scratch_shapes=[pltpu.SemaphoreType.DMA],
        compiler_params=pltpu.CompilerParams(vmem_limit_bytes=10 * 2**20),
        cost_estimate=pl.CostEstimate(
            flops=2 * total * comps * span * feats, bytes_accessed=8 * 2**20, transcendentals=0
        ),
        name="score_moved",
    )(offsets, log_det, factors, rows)


def turn_kernel(spot, mine_ref, theirs_ref, out_ref):
    span, half = out_ref.shape[0], mine_ref.shape[0]
    own = pl.multiple_of(spot[3] * span, span)
    out_ref[:, :half] = mine_ref[:, pl.ds(own, span)].T
    out_ref[:, half:] = theirs_ref[:, pl.ds(own, span)].T


def turn(spot, mine, theirs, span):
    return pl.pallas_call(
        turn_kernel,
        out_shape=pltpu.VMEM((span, 2 * mine.shape[0]), mine.dtype),
        in_specs=[SMEM, VMEM, VMEM],
        out_specs=VMEM,
        compiler_params=pltpu.CompilerParams(vmem_limit_bytes=4 * 2**20),
        name="turn",
    )(spot, mine, theirs)


def moment_kernel(spot, resp_ref, own_ref, mine_ref, theirs_ref, means_ref, cov_ref, all_means, stage, sems):
    comps, total = resp_ref.shape
    span, half = own_ref.shape[0], mine_ref.shape[0]
    feats = mine_ref.shape[1]
    core = spot[2]
    resp = jnp.concatenate(
        [
            resp_ref[:, pl.ds(pl.multiple_of(core * half, half), half)],
            resp_ref[:, pl.ds(pl.multiple_of((1 - core) * half, half), half)],
        ],
        axis=1,
    )
    inverse = 1.0 / (jnp.sum(resp, axis=1, keepdims=True) + 1.0)
    high = resp.astype(jnp.bfloat16)
    low = (resp - high.astype(jnp.float32)).astype(jnp.bfloat16)
    zero = jnp.zeros((8, total), jnp.bfloat16)

    def product(left, cols):
        right = jnp.concatenate([mine_ref[:, cols], theirs_ref[:, cols]], axis=0)
        return jnp.dot(left, right, preferred_element_type=jnp.float32)

    sums = product(jnp.concatenate([high, low, zero], axis=0), pl.ds(0, feats))
    all_means[...] = (sums[:comps] + sums[comps : 2 * comps]) * inverse
    means_ref[...] = all_means[:, pl.ds(pl.multiple_of(spot[3] * span, span), span)]
    copies = []
    for k in range(comps):
        weighted = own_ref[...].astype(jnp.float32) * resp[k : k + 1]
        own_means = jnp.sum(weighted, axis=1, keepdims=True) * inverse[k : k + 1]
        left = weighted.astype(jnp.bfloat16)
        tile = feats if k + 1 < comps else feats // 4
        for at in range(0, feats, tile):
            cols = pl.ds(at, tile)
            gram = product(left, cols)
            stage[k, :, cols] = (
                gram * inverse[k : k + 1] - own_means * all_means[k : k + 1, cols]
            ).astype(jnp.bfloat16)
            copy = pltpu.make_async_copy(stage.at[k, :, cols], cov_ref.at[k, :, cols], sems.at[len(copies)])
            copy.start()
            copies.append(copy)
    for copy in copies:
        copy.wait()


def moments(spot, resp, own, mine, theirs):
    comps, total = resp.shape
    span, feats = own.shape[0], mine.shape[1]
    return pl.pallas_call(
        moment_kernel,
        out_shape=(
            jax.ShapeDtypeStruct((comps, span), jnp.float32),
            jax.ShapeDtypeStruct((comps, span, feats), jnp.bfloat16),
        ),
        in_specs=[SMEM, VMEM, VMEM, VMEM, VMEM],
        out_specs=(VMEM, ANY),
        scratch_shapes=[
            pltpu.VMEM((comps, feats), jnp.float32),
            pltpu.VMEM((comps, span, feats), jnp.bfloat16),
            pltpu.SemaphoreType.DMA((comps + 3,)),
        ],
        compiler_params=pltpu.CompilerParams(vmem_limit_bytes=14 * 2**20),
        name="moments",
    )(spot, resp, own, mine, theirs)


def x_even(z, y, x, c):
    return (z, y, x ^ 1, c)


def x_odd(z, y, x, c):
    return (z, y, 3 - x, c)


def y_far(z, y, x, c):
    return (z, y + 2, x, c)


def y_near(z, y, x, c):
    return (z, y ^ 1, x, c)


def z_even(z, y, x, c):
    return (z ^ 1, y, x, c)


def z_odd(z, y, x, c):
    return (z + 1 if z % 2 else z - 1, y, x, c)


Z_LAST = {1: 6, 6: 1, 2: 5, 5: 2, 3: 0, 0: 3, 4: 7, 7: 4}


def z_far(z, y, x, c):
    return (Z_LAST[z], y, x, c)


def shards(samples, inverse_factors, offsets, log_weights):
    z, y, x, c = place()
    rows_here = samples.shape[0]
    spot = jnp.stack([y, x, c, lax.axis_index("narrow"), z]).astype(jnp.int32)
    span = inverse_factors.shape[1]
    log_det = log_dets(spot, inverse_factors)
    mine, log_det = gather(spot, samples, log_det)
    theirs = send(mine, core_swap)
    first = score(offsets, log_det, inverse_factors, mine)
    second, theirs = score_moved(offsets, log_det, inverse_factors, theirs)
    own = turn(spot, mine, theirs, span)
    loglik = jnp.where(
        c == 0, jnp.concatenate([first, second], axis=1), jnp.concatenate([second, first], axis=1)
    )
    for move in (x_even, x_odd, y_far):
        loglik = loglik + send(loglik, move)
    loglik = loglik + log_weights[:, None]
    peak = jnp.max(loglik, axis=0)
    total = jnp.sum(jnp.exp(loglik - peak[None, :]), axis=0)
    pair = jnp.stack([peak, total])
    for move in (core_swap, y_near, z_even, z_odd, z_far):
        other = send(pair, move)
        peak = jnp.maximum(pair[0], other[0])
        total = pair[1] * jnp.exp(pair[0] - peak) + other[1] * jnp.exp(other[0] - peak)
        pair = jnp.stack([peak, total])
    log_norm = jnp.log(pair[1])
    responsibility = jnp.exp((loglik - pair[0][None, :]) - log_norm[None, :])
    means, covariance = moments(spot, responsibility, own, mine, theirs)
    first_row = ((c * NZ + z) * 2 + y % 2) * rows_here
    own_norm = lax.dynamic_slice_in_dim(log_norm, first_row, rows_here, 0)
    return (own_norm, means, covariance)


def solution(mesh):
    return jax.shard_map(
        shards,
        mesh=mesh,
        in_specs=(P("wide", "narrow"), P("wide", "narrow", None), P("wide", "narrow"), P("wide")),
        out_specs=(P("wide"), P("wide", "narrow"), P("wide", "narrow", None)),
        check_vma=False,
    )
```

```python
import functools

import jax
import jax.numpy as jnp
from jax import lax
from jax.experimental import pallas as pl
from jax.experimental.pallas import tpu as pltpu
from jax.sharding import PartitionSpec as P

AXES = ("wide", "narrow")
NZ, NY, NX = 8, 4, 4


def linear(z, y, x, c):
    return ((z * 2 + y % 2) * 2 + c) * 8 + (y // 2) * 4 + x


def pairs(move):
    out = []
    for z in range(NZ):
        for y in range(NY):
            for x in range(NX):
                for c in range(2):
                    tz, ty, tx, tc = move(z, y, x, c)
                    out.append((linear(z, y, x, c), linear(tz % NZ, ty % NY, tx % NX, tc)))
    return out


def send(value, move):
    return lax.ppermute(value, AXES, pairs(move))


def z_step(d):
    return lambda z, y, x, c: (z + d, y, x, c)


def first_step(d):
    return lambda z, y, x, c: (z, y + d, x, c) if c == 0 else (z, y, x + d, c)


def second_step(d):
    return lambda z, y, x, c: (z, y, x + d, c) if c == 0 else (z, y + d, x, c)


def core_swap(z, y, x, c):
    return (z, y, x, 1 - c)


def place():
    w, n = lax.axis_index("wide"), lax.axis_index("narrow")
    return w // 4, (n // 4) * 2 + (w // 2) % 2, n % 4, w % 2


def column_kernel(spot, *refs):
    out_ref = refs[-1]
    for i, ref in enumerate(refs[:-1]):
        out_ref[(spot[4] + i) % NZ] = ref[...]


def make_column(spot, ring):
    return pl.pallas_call(
        column_kernel,
        out_shape=pltpu.VMEM((NZ,) + ring[0].shape, ring[0].dtype),
        in_specs=[SMEM] + [VMEM] * NZ,
        out_specs=VMEM,
        compiler_params=pltpu.CompilerParams(vmem_limit_bytes=2 * 2**20),
        name="column",
    )(spot, *ring)


def gather(spot, samples, factors, terms):
    back, ahead, back2, ahead2 = (send(samples, z_step(d)) for d in (1, -1, 2, -2))
    ahead3, back3, far = send(ahead2, z_step(-1)), send(back2, z_step(1)), send(ahead2, z_step(-2))
    column = make_column(spot, [samples, ahead, ahead2, ahead3, far, back3, back2, back])
    column, terms = lax.optimization_barrier((column, terms))
    before, after, across = (send(column, first_step(d)) for d in (1, -1, 2))
    low, high = jnp.stack([column, after]), jnp.stack([across, before])
    before_low = send(low, second_step(1))
    after_high = send(high, second_step(-1))
    before_high = send(high, second_step(1))
    after_low = send(low, second_step(-1))
    far_low = send(before_low, second_step(1))
    far_high = send(after_high, second_step(-1))
    near = [low, high, before_low, after_high, before_high, after_low]
    near_rows = lay(spot, NEAR, None, near)
    *held, mark = hold(*factors, near_rows)
    return lay(spot, FAR, near_rows, [far_low, far_high], [mark]), held, terms


NEAR = ((0, 0, 2), (0, 2, 2), (3, 0, 2), (1, 2, 2), (3, 2, 2), (1, 0, 2))
FAR = ((2, 0, 2), (2, 2, 2))
VMEM = pl.BlockSpec(memory_space=pltpu.VMEM)
ANY = pl.BlockSpec(memory_space=pl.ANY)
SMEM = pl.BlockSpec(memory_space=pltpu.SMEM)


def lay_kernel(places, has_rows, spot, *refs):
    parts = refs[has_rows : has_rows + len(places)]
    rows, sems = refs[-2:]
    here_y, here_x = spot[0], spot[1]
    core = spot[2]
    blocks = rows.reshape(NZ, 2, 48, rows.shape[1])
    copies = []
    for part, (second, first, many) in zip(parts, places, strict=True):
        for i in range(many):
            ay, ax = (here_y + first + i) % 4, (here_x + second) % 4
            by, bx = (here_y + second) % 4, (here_x + first + i) % 4
            at_y = jnp.where(core == 0, ay, by)
            at_x = jnp.where(core == 0, ax, bx)
            col = pl.multiple_of(((at_y // 2) * 4 + at_x) * 256, 256)
            copy = pltpu.make_async_copy(
                part.at[i], blocks.at[:, at_y % 2, :, pl.ds(col, 256)], sems.at[len(copies)]
            )
            copy.start()
            copies.append(copy)
    for copy in copies:
        copy.wait()


def lay(spot, places, rows, parts, after=()):
    has_rows = 0 if rows is None else 1
    return pl.pallas_call(
        functools.partial(lay_kernel, places, has_rows),
        out_shape=pltpu.VMEM((768, 2048), jnp.bfloat16),
        in_specs=[SMEM] + [VMEM] * has_rows + [ANY] * (len(parts) + len(after)),
        out_specs=VMEM,
        scratch_shapes=[pltpu.SemaphoreType.DMA((12,))],
        input_output_aliases={1: 0} if has_rows else {},
        compiler_params=pltpu.CompilerParams(vmem_limit_bytes=2 * 2**20),
        name="lay",
    )(spot, *([rows] if has_rows else []), *parts, *after)


def hold_kernel(first, second, _, first_out, second_out, mark, sems):
    copies = [
        pltpu.make_async_copy(first, first_out, sems.at[0]),
        pltpu.make_async_copy(second, second_out, sems.at[1]),
    ]
    for copy in copies:
        copy.start()
    mark[...] = jnp.zeros_like(mark)
    for copy in copies:
        copy.wait()


def hold(first, second, after):
    kept = pltpu.VMEM(first.shape, first.dtype)
    return pl.pallas_call(
        hold_kernel,
        out_shape=(kept, kept, jax.ShapeDtypeStruct((8, 128), jnp.float32)),
        in_specs=[ANY, ANY, ANY],
        out_specs=(VMEM, VMEM, VMEM),
        scratch_shapes=[pltpu.SemaphoreType.DMA((2,))],
        compiler_params=pltpu.CompilerParams(vmem_limit_bytes=2 * 2**20),
        name="hold",
    )(first, second, after)


def score_kernel(spot, terms_ref, their_terms_ref, factors_ref, their_factors_ref, rows_ref, partial_ref):
    comps, span, feats = factors_ref.shape
    own = pl.multiple_of(spot[3] * span, span)
    eye = lax.broadcasted_iota(jnp.int32, (span, span), 0) == lax.broadcasted_iota(
        jnp.int32, (span, span), 1
    )
    for group, (factors, terms) in enumerate(((factors_ref, terms_ref), (their_factors_ref, their_terms_ref))):
        offsets = terms[:, :span].T
        projected = lax.dot_general(
            factors[...].reshape(comps * span, feats),
            rows_ref[...],
            (((1,), (1,)), ((), ())),
            preferred_element_type=jnp.float32,
        )
        for k in range(comps):
            square = factors[k, :, pl.ds(own, span)].astype(jnp.float32)
            diag = jnp.sum(jnp.where(eye, square, 0.0), axis=1, keepdims=True)
            log_det = jnp.sum(jnp.log(diag), axis=0, keepdims=True)
            centered = projected[k * span : (k + 1) * span] - offsets[:, k : k + 1]
            quadratic = jnp.sum(centered * centered, axis=0, keepdims=True)
            at = group * comps + k
            partial_ref[at : at + 1, :] = log_det - 0.5 * quadratic


def score(spot, terms, their_terms, factors, their_factors, rows):
    comps, span, feats = factors.shape
    total = rows.shape[0]
    return pl.pallas_call(
        score_kernel,
        out_shape=jax.ShapeDtypeStruct((2 * comps, total), jnp.float32),
        in_specs=[SMEM, VMEM, VMEM, VMEM, VMEM, VMEM],
        out_specs=VMEM,
        compiler_params=pltpu.CompilerParams(vmem_limit_bytes=14 * 2**20),
        cost_estimate=pl.CostEstimate(
            flops=4 * total * comps * span * feats, bytes_accessed=8 * 2**20, transcendentals=0
        ),
        name="score",
    )(spot, terms, their_terms, factors, their_factors, rows)


def turn_kernel(spot, mine_ref, theirs_ref, _, out_ref, held, sem):
    span, half = out_ref.shape[0], mine_ref.shape[0]
    own = pl.multiple_of(spot[3] * span, span)
    copy = pltpu.make_async_copy(theirs_ref, held, sem)
    copy.start()
    out_ref[:, :half] = mine_ref[:, pl.ds(own, span)].T
    copy.wait()
    out_ref[:, half:] = held[:, pl.ds(own, span)].T


def turn(spot, mine, theirs, span, after):
    return pl.pallas_call(
        turn_kernel,
        out_shape=(
            pltpu.VMEM((span, 2 * mine.shape[0]), mine.dtype),
            pltpu.VMEM(theirs.shape, theirs.dtype),
        ),
        in_specs=[SMEM, VMEM, ANY, ANY],
        out_specs=(VMEM, VMEM),
        scratch_shapes=[pltpu.SemaphoreType.DMA],
        compiler_params=pltpu.CompilerParams(vmem_limit_bytes=4 * 2**20),
        cost_estimate=pl.CostEstimate(flops=0, bytes_accessed=8 * 2**20, transcendentals=0),
        name="turn",
    )(spot, mine, theirs, after)


def moment_kernel(
    spot, loglik_ref, their_loglik_ref, norms_ref, their_norms_ref, own_ref, mine_ref, theirs_ref,
    norm_ref, means_ref, cov_ref, all_means, stage, sems,
):
    comps, half = loglik_ref.shape
    span, total = own_ref.shape
    feats = mine_ref.shape[1]
    turned = pltpu.roll(jnp.broadcast_to(norms_ref[1:2], (8, half)), lax.rem(half - spot[5], half), 1)
    norm_ref[...] = turned[0:1, : norm_ref.shape[1]]
    resp = jnp.concatenate(
        [
            jnp.exp((loglik_ref[...] - norms_ref[0:1]) - norms_ref[1:2]),
            jnp.exp((their_loglik_ref[...] - their_norms_ref[0:1]) - their_norms_ref[1:2]),
        ],
        axis=1,
    )
    inverse = 1.0 / (jnp.sum(resp, axis=1, keepdims=True) + 1.0)
    high = resp.astype(jnp.bfloat16)
    low = (resp - high.astype(jnp.float32)).astype(jnp.bfloat16)
    zero = jnp.zeros((8, total), jnp.bfloat16)

    def product(left, cols):
        right = jnp.concatenate([mine_ref[:, cols], theirs_ref[:, cols]], axis=0)
        return jnp.dot(left, right, preferred_element_type=jnp.float32)

    sums = product(jnp.concatenate([high, low, zero], axis=0), pl.ds(0, feats))
    all_means[...] = (sums[:comps] + sums[comps : 2 * comps]) * inverse
    means_ref[...] = all_means[:, pl.ds(pl.multiple_of(spot[3] * span, span), span)]
    copies = []
    for k in range(comps):
        weighted = own_ref[...].astype(jnp.float32) * resp[k : k + 1]
        own_means = jnp.sum(weighted, axis=1, keepdims=True) * inverse[k : k + 1]
        left = weighted.astype(jnp.bfloat16)
        tile = feats if k + 1 < comps else feats // 4
        for at in range(0, feats, tile):
            cols = pl.ds(at, tile)
            gram = product(left, cols)
            stage[k, :, cols] = (
                gram * inverse[k : k + 1] - own_means * all_means[k : k + 1, cols]
            ).astype(jnp.bfloat16)
            copy = pltpu.make_async_copy(stage.at[k, :, cols], cov_ref.at[k, :, cols], sems.at[len(copies)])
            copy.start()
            copies.append(copy)
    for copy in copies:
        copy.wait()


def moments(spot, loglik, their_loglik, norms, their_norms, own, mine, theirs, rows_here):
    comps = loglik.shape[0]
    span, feats = own.shape[0], mine.shape[1]
    return pl.pallas_call(
        moment_kernel,
        out_shape=(
            jax.ShapeDtypeStruct((1, rows_here), jnp.float32),
            jax.ShapeDtypeStruct((comps, span), jnp.float32),
            jax.ShapeDtypeStruct((comps, span, feats), jnp.bfloat16),
        ),
        in_specs=[SMEM] + [VMEM] * 7,
        out_specs=(VMEM, VMEM, ANY),
        scratch_shapes=[
            pltpu.VMEM((comps, feats), jnp.float32),
            pltpu.VMEM((comps, span, feats), jnp.bfloat16),
            pltpu.SemaphoreType.DMA((comps + 3,)),
        ],
        compiler_params=pltpu.CompilerParams(vmem_limit_bytes=14 * 2**20),
        name="moments",
    )(spot, loglik, their_loglik, norms, their_norms, own, mine, theirs)


def x_even(z, y, x, c):
    return (z, y, x ^ 1, c)


def x_odd(z, y, x, c):
    return (z, y, 3 - x, c)


def y_far(z, y, x, c):
    return (z, y + 2, x, c)


def y_near(z, y, x, c):
    return (z, y ^ 1, x, c)


def z_even(z, y, x, c):
    return (z ^ 1, y, x, c)


def z_odd(z, y, x, c):
    return (z + 1 if z % 2 else z - 1, y, x, c)


Z_LAST = {1: 6, 6: 1, 2: 5, 5: 2, 3: 0, 0: 3, 4: 7, 7: 4}


def z_far(z, y, x, c):
    return (Z_LAST[z], y, x, c)


def shards(samples, inverse_factors, offsets, log_weights):
    z, y, x, c = place()
    rows_here = samples.shape[0]
    comps, span, _ = inverse_factors.shape
    first_row = (z * 2 + y % 2) * rows_here
    spot = jnp.stack([y, x, c, lax.axis_index("narrow"), z, first_row]).astype(jnp.int32)
    terms = jnp.concatenate([offsets, jnp.broadcast_to(log_weights[:, None], (comps, 128))], axis=1)
    their_factors = send(inverse_factors, core_swap)
    their_terms = send(terms, core_swap)
    mine, held, (terms, their_terms) = gather(spot, samples, (inverse_factors, their_factors), (terms, their_terms))
    theirs = send(mine, core_swap)
    loglik = score(spot, terms, their_terms, *held, mine)
    for move in (x_even, x_odd, y_far):
        loglik = loglik + send(loglik, move)
    loglik = loglik + jnp.concatenate([terms[:, span:], their_terms[:, span:]], axis=0)[:, :1]
    their_loglik = send(loglik[comps:], core_swap)
    peak = jnp.max(loglik, axis=0)
    total = jnp.sum(jnp.exp(loglik - peak[None, :]), axis=0)
    for move in (y_near, z_even, z_odd, z_far):
        pair = jnp.stack([peak, total])
        if move is z_far:
            own, theirs = turn(spot, mine, theirs, span, pair)
        got = send(pair, move)
        peak = jnp.maximum(pair[0], got[0])
        total = pair[1] * jnp.exp(pair[0] - peak) + got[1] * jnp.exp(got[0] - peak)
    norms = jnp.stack([peak, jnp.log(total)])
    their_norms = send(norms, core_swap)
    norm, means, covariance = moments(
        spot, loglik[:comps], their_loglik, norms, their_norms, own, mine, theirs, rows_here
    )
    return (norm.reshape(rows_here), means, covariance)


def solution(mesh):
    return jax.shard_map(
        shards,
        mesh=mesh,
        in_specs=(P("wide", "narrow"), P("wide", "narrow", None), P("wide", "narrow"), P("wide")),
        out_specs=(P("wide"), P("wide", "narrow"), P("wide", "narrow", None)),
        check_vma=False,
    )
```

```python
import functools

import jax
import jax.numpy as jnp
from jax import lax
from jax.experimental import pallas as pl
from jax.experimental.pallas import tpu as pltpu
from jax.sharding import PartitionSpec as P

AXES = ("wide", "narrow")
NZ, NY, NX = 8, 4, 4


def linear(z, y, x, c):
    return ((z * 2 + y % 2) * 2 + c) * 8 + (y // 2) * 4 + x


def pairs(move):
    out = []
    for z in range(NZ):
        for y in range(NY):
            for x in range(NX):
                for c in range(2):
                    tz, ty, tx, tc = move(z, y, x, c)
                    out.append((linear(z, y, x, c), linear(tz % NZ, ty % NY, tx % NX, tc)))
    return out


def send(value, move):
    return lax.ppermute(value, AXES, pairs(move))


def z_step(d):
    return lambda z, y, x, c: (z + d, y, x, c)


def first_step(d):
    return lambda z, y, x, c: (z, y + d, x, c) if c == 0 else (z, y, x + d, c)


def second_step(d):
    return lambda z, y, x, c: (z, y, x + d, c) if c == 0 else (z, y + d, x, c)


def core_swap(z, y, x, c):
    return (z, y, x, 1 - c)


def place():
    w, n = lax.axis_index("wide"), lax.axis_index("narrow")
    return w // 4, (n // 4) * 2 + (w // 2) % 2, n % 4, w % 2


def column_kernel(spot, *refs):
    out_ref = refs[-1]
    for i, ref in enumerate(refs[:-1]):
        out_ref[(spot[4] + i) % NZ] = ref[...]


def make_column(spot, ring):
    return pl.pallas_call(
        column_kernel,
        out_shape=pltpu.VMEM((NZ,) + ring[0].shape, ring[0].dtype),
        in_specs=[SMEM] + [VMEM] * NZ,
        out_specs=VMEM,
        compiler_params=pltpu.CompilerParams(vmem_limit_bytes=2 * 2**20),
        name="column",
    )(spot, *ring)


def gather(spot, samples, factors, terms):
    back, ahead, back2, ahead2 = (send(samples, z_step(d)) for d in (1, -1, 2, -2))
    ahead3, back3, far = send(ahead2, z_step(-1)), send(back2, z_step(1)), send(ahead2, z_step(-2))
    column = make_column(spot, [samples, ahead, ahead2, ahead3, far, back3, back2, back])
    column, terms = lax.optimization_barrier((column, terms))
    before, after, across = (send(column, first_step(d)) for d in (1, -1, 2))
    low, high = jnp.stack([column, after]), jnp.stack([across, before])
    before_low = send(low, second_step(1))
    after_high = send(high, second_step(-1))
    before_high = send(high, second_step(1))
    after_low = send(low, second_step(-1))
    far_low = send(before_low, second_step(1))
    far_high = send(after_high, second_step(-1))
    near = [low, high, before_low, after_high, before_high, after_low]
    near_rows = lay(spot, NEAR, None, near)
    *held, log_det = hold(spot, *factors, near_rows)
    return lay(spot, FAR, near_rows, [far_low, far_high], [log_det]), [log_det, *held], terms


NEAR = ((0, 0, 2), (0, 2, 2), (3, 0, 2), (1, 2, 2), (3, 2, 2), (1, 0, 2))
FAR = ((2, 0, 2), (2, 2, 2))
VMEM = pl.BlockSpec(memory_space=pltpu.VMEM)
ANY = pl.BlockSpec(memory_space=pl.ANY)
SMEM = pl.BlockSpec(memory_space=pltpu.SMEM)


def lay_kernel(places, has_rows, spot, *refs):
    parts = refs[has_rows : has_rows + len(places)]
    rows, sems = refs[-2:]
    here_y, here_x = spot[0], spot[1]
    core = spot[2]
    blocks = rows.reshape(NZ, 2, 48, rows.shape[1])
    copies = []
    for part, (second, first, many) in zip(parts, places, strict=True):
        for i in range(many):
            ay, ax = (here_y + first + i) % 4, (here_x + second) % 4
            by, bx = (here_y + second) % 4, (here_x + first + i) % 4
            at_y = jnp.where(core == 0, ay, by)
            at_x = jnp.where(core == 0, ax, bx)
            col = pl.multiple_of(((at_y // 2) * 4 + at_x) * 256, 256)
            copy = pltpu.make_async_copy(
                part.at[i], blocks.at[:, at_y % 2, :, pl.ds(col, 256)], sems.at[len(copies)]
            )
            copy.start()
            copies.append(copy)
    for copy in copies:
        copy.wait()


def lay(spot, places, rows, parts, after=()):
    has_rows = 0 if rows is None else 1
    return pl.pallas_call(
        functools.partial(lay_kernel, places, has_rows),
        out_shape=pltpu.VMEM((768, 2048), jnp.bfloat16),
        in_specs=[SMEM] + [VMEM] * has_rows + [ANY] * (len(parts) + len(after)),
        out_specs=VMEM,
        scratch_shapes=[pltpu.SemaphoreType.DMA((12,))],
        input_output_aliases={1: 0} if has_rows else {},
        compiler_params=pltpu.CompilerParams(vmem_limit_bytes=2 * 2**20),
        name="lay",
    )(spot, *([rows] if has_rows else []), *parts, *after)


def hold_kernel(spot, first, second, _, first_out, second_out, log_det_ref, sems):
    copies = [
        pltpu.make_async_copy(first, first_out, sems.at[0]),
        pltpu.make_async_copy(second, second_out, sems.at[1]),
    ]
    for copy in copies:
        copy.start()
    comps, span, _ = first_out.shape
    own = pl.multiple_of(spot[3] * span, span)
    eye = lax.broadcasted_iota(jnp.int32, (span, span), 0) == lax.broadcasted_iota(
        jnp.int32, (span, span), 1
    )
    for copy in copies:
        copy.wait()
    for group, factors in enumerate((first_out, second_out)):
        for k in range(comps):
            square = factors[k, :, pl.ds(own, span)].astype(jnp.float32)
            diag = jnp.sum(jnp.where(eye, square, 0.0), axis=1, keepdims=True)
            total = jnp.sum(jnp.log(diag), axis=0, keepdims=True)
            at = group * comps + k
            log_det_ref[at : at + 1, :] = jnp.broadcast_to(total, (1, log_det_ref.shape[1]))


def hold(spot, first, second, after):
    kept = pltpu.VMEM(first.shape, first.dtype)
    return pl.pallas_call(
        hold_kernel,
        out_shape=(kept, kept, jax.ShapeDtypeStruct((2 * first.shape[0], 128), jnp.float32)),
        in_specs=[SMEM, ANY, ANY, ANY],
        out_specs=(VMEM, VMEM, VMEM),
        scratch_shapes=[pltpu.SemaphoreType.DMA((2,))],
        compiler_params=pltpu.CompilerParams(vmem_limit_bytes=2 * 2**20),
        name="hold",
    )(spot, first, second, after)


def score_kernel(terms_ref, their_terms_ref, log_det_ref, factors_ref, their_factors_ref, rows_ref, partial_ref):
    comps, span, feats = factors_ref.shape
    for group, (factors, terms) in enumerate(((factors_ref, terms_ref), (their_factors_ref, their_terms_ref))):
        offsets = terms[:, :span].T
        projected = lax.dot_general(
            factors[...].reshape(comps * span, feats),
            rows_ref[...],
            (((1,), (1,)), ((), ())),
            preferred_element_type=jnp.float32,
        )
        for k in range(comps):
            centered = projected[k * span : (k + 1) * span] - offsets[:, k : k + 1]
            quadratic = jnp.sum(centered * centered, axis=0, keepdims=True)
            at = group * comps + k
            partial_ref[at : at + 1, :] = log_det_ref[at : at + 1, 0:1] - 0.5 * quadratic


def score(terms, their_terms, log_det, factors, their_factors, rows):
    comps, span, feats = factors.shape
    total = rows.shape[0]
    return pl.pallas_call(
        score_kernel,
        out_shape=jax.ShapeDtypeStruct((2 * comps, total), jnp.float32),
        in_specs=[VMEM] * 6,
        out_specs=VMEM,
        compiler_params=pltpu.CompilerParams(vmem_limit_bytes=14 * 2**20),
        cost_estimate=pl.CostEstimate(
            flops=4 * total * comps * span * feats, bytes_accessed=8 * 2**20, transcendentals=0
        ),
        name="score",
    )(terms, their_terms, log_det, factors, their_factors, rows)


def turn_kernel(spot, mine_ref, theirs_ref, _, out_ref, held, sem):
    span, half = out_ref.shape[0], mine_ref.shape[0]
    own = pl.multiple_of(spot[3] * span, span)
    copy = pltpu.make_async_copy(theirs_ref, held, sem)
    copy.start()
    out_ref[:, :half] = mine_ref[:, pl.ds(own, span)].T
    copy.wait()
    out_ref[:, half:] = held[:, pl.ds(own, span)].T


def turn(spot, mine, theirs, span, after):
    return pl.pallas_call(
        turn_kernel,
        out_shape=(
            pltpu.VMEM((span, 2 * mine.shape[0]), mine.dtype),
            pltpu.VMEM(theirs.shape, theirs.dtype),
        ),
        in_specs=[SMEM, VMEM, ANY, ANY],
        out_specs=(VMEM, VMEM),
        scratch_shapes=[pltpu.SemaphoreType.DMA],
        compiler_params=pltpu.CompilerParams(vmem_limit_bytes=4 * 2**20),
        cost_estimate=pl.CostEstimate(flops=0, bytes_accessed=8 * 2**20, transcendentals=0),
        name="turn",
    )(spot, mine, theirs, after)


def moment_kernel(
    spot, loglik_ref, their_loglik_ref, norms_ref, their_norms_ref, own_ref, mine_ref, theirs_ref,
    norm_ref, means_ref, cov_ref, all_means, stage, sems,
):
    comps, half = loglik_ref.shape
    span, total = own_ref.shape
    feats = mine_ref.shape[1]
    turned = pltpu.roll(jnp.broadcast_to(norms_ref[1:2], (8, half)), lax.rem(half - spot[5], half), 1)
    norm_ref[...] = turned[0:1, : norm_ref.shape[1]]
    resp = jnp.concatenate(
        [
            jnp.exp((loglik_ref[...] - norms_ref[0:1]) - norms_ref[1:2]),
            jnp.exp((their_loglik_ref[...] - their_norms_ref[0:1]) - their_norms_ref[1:2]),
        ],
        axis=1,
    )
    inverse = 1.0 / (jnp.sum(resp, axis=1, keepdims=True) + 1.0)
    high = resp.astype(jnp.bfloat16)
    low = (resp - high.astype(jnp.float32)).astype(jnp.bfloat16)
    zero = jnp.zeros((8, total), jnp.bfloat16)

    def product(left, cols):
        right = jnp.concatenate([mine_ref[:, cols], theirs_ref[:, cols]], axis=0)
        return jnp.dot(left, right, preferred_element_type=jnp.float32)

    sums = product(jnp.concatenate([high, low, zero], axis=0), pl.ds(0, feats))
    all_means[...] = (sums[:comps] + sums[comps : 2 * comps]) * inverse
    means_ref[...] = all_means[:, pl.ds(pl.multiple_of(spot[3] * span, span), span)]
    copies = []
    for k in range(comps):
        weighted = own_ref[...].astype(jnp.float32) * resp[k : k + 1]
        own_means = jnp.sum(weighted, axis=1, keepdims=True) * inverse[k : k + 1]
        left = weighted.astype(jnp.bfloat16)
        tile = feats if k + 1 < comps else feats // 4
        for at in range(0, feats, tile):
            cols = pl.ds(at, tile)
            gram = product(left, cols)
            stage[k, :, cols] = (
                gram * inverse[k : k + 1] - own_means * all_means[k : k + 1, cols]
            ).astype(jnp.bfloat16)
            copy = pltpu.make_async_copy(stage.at[k, :, cols], cov_ref.at[k, :, cols], sems.at[len(copies)])
            copy.start()
            copies.append(copy)
    for copy in copies:
        copy.wait()


def moments(spot, loglik, their_loglik, norms, their_norms, own, mine, theirs, rows_here):
    comps = loglik.shape[0]
    span, feats = own.shape[0], mine.shape[1]
    return pl.pallas_call(
        moment_kernel,
        out_shape=(
            jax.ShapeDtypeStruct((1, rows_here), jnp.float32),
            jax.ShapeDtypeStruct((comps, span), jnp.float32),
            jax.ShapeDtypeStruct((comps, span, feats), jnp.bfloat16),
        ),
        in_specs=[SMEM] + [VMEM] * 7,
        out_specs=(VMEM, VMEM, ANY),
        scratch_shapes=[
            pltpu.VMEM((comps, feats), jnp.float32),
            pltpu.VMEM((comps, span, feats), jnp.bfloat16),
            pltpu.SemaphoreType.DMA((comps + 3,)),
        ],
        compiler_params=pltpu.CompilerParams(vmem_limit_bytes=14 * 2**20),
        name="moments",
    )(spot, loglik, their_loglik, norms, their_norms, own, mine, theirs)


def x_even(z, y, x, c):
    return (z, y, x ^ 1, c)


def x_odd(z, y, x, c):
    return (z, y, 3 - x, c)


def y_far(z, y, x, c):
    return (z, y + 2, x, c)


def y_near(z, y, x, c):
    return (z, y ^ 1, x, c)


def z_even(z, y, x, c):
    return (z ^ 1, y, x, c)


def z_odd(z, y, x, c):
    return (z + 1 if z % 2 else z - 1, y, x, c)


Z_LAST = {1: 6, 6: 1, 2: 5, 5: 2, 3: 0, 0: 3, 4: 7, 7: 4}


def z_far(z, y, x, c):
    return (Z_LAST[z], y, x, c)


def shards(samples, inverse_factors, offsets, log_weights):
    z, y, x, c = place()
    rows_here = samples.shape[0]
    comps, span, _ = inverse_factors.shape
    first_row = (z * 2 + y % 2) * rows_here
    spot = jnp.stack([y, x, c, lax.axis_index("narrow"), z, first_row]).astype(jnp.int32)
    terms = jnp.concatenate([offsets, jnp.broadcast_to(log_weights[:, None], (comps, 128))], axis=1)
    their_factors = send(inverse_factors, core_swap)
    their_terms = send(terms, core_swap)
    mine, held, (terms, their_terms) = gather(spot, samples, (inverse_factors, their_factors), (terms, their_terms))
    theirs = send(mine, core_swap)
    loglik = score(terms, their_terms, *held, mine)
    for move in (x_even, x_odd, y_far):
        loglik = loglik + send(loglik, move)
    loglik = loglik + jnp.concatenate([terms[:, span:], their_terms[:, span:]], axis=0)[:, :1]
    their_loglik = send(loglik[comps:], core_swap)
    peak = jnp.max(loglik, axis=0)
    total = jnp.sum(jnp.exp(loglik - peak[None, :]), axis=0)
    for move in (y_near, z_even, z_odd, z_far):
        pair = jnp.stack([peak, total])
        if move is z_far:
            own, theirs = turn(spot, mine, theirs, span, pair)
        got = send(pair, move)
        peak = jnp.maximum(pair[0], got[0])
        total = pair[1] * jnp.exp(pair[0] - peak) + got[1] * jnp.exp(got[0] - peak)
    norms = jnp.stack([peak, jnp.log(total)])
    their_norms = send(norms, core_swap)
    norm, means, covariance = moments(
        spot, loglik[:comps], their_loglik, norms, their_norms, own, mine, theirs, rows_here
    )
    return (norm.reshape(rows_here), means, covariance)


def solution(mesh):
    return jax.shard_map(
        shards,
        mesh=mesh,
        in_specs=(P("wide", "narrow"), P("wide", "narrow", None), P("wide", "narrow"), P("wide")),
        out_specs=(P("wide"), P("wide", "narrow"), P("wide", "narrow", None)),
        check_vma=False,
    )
```
